128 devices in a mesh: sim: 2 (over x_hi), tm: 64 (over y, z, x_lo, core).
Axes of the slice: x: 4 (x_hi: 2, x_lo: 2; x = x_hi * 2 + x_lo), y: 4, z: 4, core: 2. Of those that a mesh axis runs over, the one named last changes fastest.
Arguments:
- strain: bfloat16 [3, 1048576], P(None, ('sim', 'tm')), parts along dimension 1, may hold values from -40 to 40, as said below
- stem_weight: bfloat16 [768, 48], replicated, may hold values from -6 to 6
- norm_gain: float32 [768], replicated, may hold values from 0.1 to 1.9
- qkv_weight: bfloat16 [768, 1152], replicated, may hold values from -3 to 3
- out_weight: bfloat16 [768, 768], replicated, may hold values from -0.21875 to 0.21875
- cotangent: bfloat16 [65536, 768], P(('sim', 'tm')), parts along dimension 0, may hold values from -6 to 6
Outputs:
- grad_qkv: float32 [1536, 1152], P(('sim', 'tm')), parts along dimension 0
- grad_out: float32 [1536, 768], P(('sim', 'tm')), parts along dimension 0
- grad_stem: float32 [1536, 48], P(('sim', 'tm')), parts along dimension 0
- grad_gain: float32 [1536], P(('sim', 'tm')), parts along dimension 0
The draws below stay inside these ranges and needn't reach their ends.
There are 2 independent parts, one for each index of `sim`. The reference program is written for one: setup_inputs(seed, part) draws one part's arguments, and reference() takes and returns one part's arrays. A program takes and returns all parts, laid end to end along the dimension named above; an argument that names none is the same for every part. Nothing has to cross between parts.
Inputs may be any that keep to these rules, and one draw needn't show every extreme that they name: `strain`: strain samples of one evolution.
All inputs are finite; a program needn't handle non-finite values.
Results may differ from the reference program's by a relative error of at most 0.0065.
The reference program's roundings to bfloat16 on the way count: a program that leaves them out, or rounds other values in their place, can miss the bound.
Values may be sent and summed in bfloat16 or wider, within the bound.
No kernel may reach another device: no remote copies, remote signals or barrier semaphores. Data moves between devices by JAX's collectives and lax.ppermute only.
A program may use at most 64 MiB of HBM per device.

```python
import math
import jax
import jax.numpy as jnp
from jax import lax

D = 768
QUERY_HEAD_COUNT = 12
KEY_VALUE_HEADS = 3
HEAD_SIZE = 64
CH = 3
STRIDE = 16
TOKENS_PER_SHARD = 512
PATCH = 48
QKV = 1152
TOKENS = 32768
N_TM = 64


def draw_strain(key, part):
    noise_key, scale_key = jax.random.split(key)
    noise_part = jax.random.truncated_normal(noise_key, -4.0, 4.0, (CH, TOKENS, STRIDE), jnp.float32)
    scale_rows = jnp.exp(jax.random.uniform(scale_key, (1, TOKENS, 1), jnp.float32, 0.0, math.log(10.0)))
    return (noise_part * scale_rows).reshape(CH, TOKENS * STRIDE).astype(jnp.bfloat16)


def draw_stem_weight(key, part):
    noise_key, scale_key = jax.random.split(key)
    noise_part = jax.random.truncated_normal(noise_key, -4.0, 4.0, (D, PATCH), jnp.float32)
    scale_rows = jnp.exp(jax.random.uniform(scale_key, (D, 1), jnp.float32, 0.0, math.log(10.0)))
    return (noise_part * scale_rows * PATCH ** (-0.5)).astype(jnp.bfloat16)


def draw_qkv_weight(key, part):
    matrix = jax.random.truncated_normal(key, -4.0, 4.0, (D, QKV), jnp.float32) * D ** (-0.5)
    return matrix.astype(jnp.bfloat16)


def strengthened(result, stream_key, source, target, shards_of, factor):
    owner, partner = [(jnp.arange(result.shape[dim]) // (result.shape[dim] // shards_of)).reshape([-1 if axis == dim else 1 for axis in range(result.ndim)]) for dim in (source, target)]
    chosen = jax.random.permutation(stream_key, shards_of)[partner]
    strong = (owner == chosen) | (owner == (partner + shards_of // 2) % shards_of)
    return jnp.where(strong, factor * result, result)


def levels(rng, dims, cuts, smallest, high):
    def one(position, blocks):
        heights = jax.random.uniform(jax.random.fold_in(jax.random.fold_in(rng, 6), position), (blocks,), jnp.float32, smallest / len(cuts), high / len(cuts))
        return jnp.repeat(jnp.exp(heights), dims[position] // blocks).reshape((-1,) + (1,) * (len(dims) - position - 1))

    level = one(*cuts[0])
    for cut in cuts[1:]:
        level = level * one(*cut)
    return level


def normal_values(stream_key, extent, spread, most, cuts=(), held_as=jnp.bfloat16):
    loudness = levels(stream_key, extent, cuts, -0.22, 0.18) if cuts else 1.0
    values = jax.random.normal(stream_key, extent, jnp.float32) * spread * loudness
    return jnp.minimum(jnp.maximum(values, -most), most).astype(held_as)


def noise_with(key, shape, scale, limit, pieces, heavy, kind=jnp.bfloat16):
    result = scale * jax.random.normal(key, shape, jnp.float32)
    if pieces:
        result = result * levels(key, shape, pieces, -0.22, 0.18)
    return jnp.clip(strengthened(result, jax.random.fold_in(key, 3), *heavy), -limit, limit).astype(kind)


def setup_inputs(seed: int = 0, part: int = 0) -> dict:
    arg_keys = jax.random.split(jax.random.key(seed), 7)
    part_keys = jax.random.split(jax.random.fold_in(arg_keys[6], part), 7)
    strain = draw_strain(jax.random.fold_in(jax.random.fold_in(arg_keys[6], part), 71), part)
    stem_weight = draw_stem_weight(jax.random.fold_in(arg_keys[6], 71), part)
    norm_gain = jnp.clip(1.0 + 0.18 * jax.random.normal(arg_keys[2], (D,), jnp.float32), 0.1, 1.9)
    qkv_weight = draw_qkv_weight(jax.random.fold_in(arg_keys[6], 71), part)
    out_weight = normal_values(arg_keys[4], (D, D), D ** -0.5, 0.21875)
    cotangent = noise_with(part_keys[5], (TOKENS, D), 0.25, 6.0, ((0, 64),), (0, 1, 64, 4.0))
    return dict(strain=strain, stem_weight=stem_weight, norm_gain=norm_gain, qkv_weight=qkv_weight, out_weight=out_weight, cotangent=cotangent)


EPSILON = 1e-05

def embed_strain(strain, stem_weight, norm_gain):
    blocks = strain.astype(jnp.float32).reshape(CH, -1, STRIDE)
    kernel = stem_weight.astype(jnp.float32).reshape(D, CH, STRIDE)
    features = jnp.einsum('cts,dcs->td', blocks, kernel, precision=lax.Precision.HIGHEST)
    inverse_rms = lax.rsqrt(lax.optimization_barrier(jnp.mean(features * features, axis=-1)) + EPSILON)
    normed = (features * inverse_rms[:, None] * norm_gain).astype(jnp.bfloat16)
    return (blocks, features, inverse_rms, normed)

def attend_block(inputs):
    query_matrix, key_rows, value_rows, attention_gradient = inputs
    row_count = query_matrix.shape[0]
    query_float = query_matrix.astype(jnp.float32)
    key_float = key_rows.astype(jnp.float32)
    value_float = value_rows.astype(jnp.float32)
    grad_float = attention_gradient.astype(jnp.float32)
    high = lax.Precision.HIGHEST
    scores = jnp.einsum('tgjd,sgd->gjts', query_float, key_float, precision=high) * HEAD_SIZE ** (-0.5)
    row_max = lax.optimization_barrier(jnp.max(scores, axis=-1, keepdims=True))
    weights = jnp.exp(scores - row_max)
    probs = weights / lax.optimization_barrier(jnp.sum(weights, axis=-1, keepdims=True))
    probs_low = lax.optimization_barrier(probs.astype(jnp.bfloat16)).astype(jnp.float32)
    mixed = jnp.einsum('gjts,sgd->tgjd', probs_low, value_float, precision=high).astype(jnp.bfloat16)
    grad_probs = jnp.einsum('tgjd,sgd->gjts', grad_float, value_float, precision=high)
    delta = lax.optimization_barrier(jnp.sum(probs * grad_probs, axis=-1, keepdims=True))
    grad_scores = lax.optimization_barrier((probs * (grad_probs - delta)).astype(jnp.bfloat16)).astype(jnp.float32)
    grad_query = (jnp.einsum('gjts,sgd->tgjd', grad_scores, key_float, precision=high) * HEAD_SIZE ** (-0.5)).astype(jnp.bfloat16)
    grad_keys = jnp.einsum('gjts,tgjd->sgd', grad_scores, query_float, precision=high) * HEAD_SIZE ** (-0.5)
    grad_values = jnp.einsum('gjts,tgjd->sgd', probs_low, grad_float, precision=high)
    return (mixed.reshape(row_count, -1), grad_query.reshape(row_count, -1), grad_keys[:row_count].reshape(row_count, -1).astype(jnp.bfloat16), grad_keys[row_count:].reshape(row_count, -1).astype(jnp.bfloat16), grad_values[:row_count].reshape(row_count, -1).astype(jnp.bfloat16), grad_values[row_count:].reshape(row_count, -1).astype(jnp.bfloat16))

def reference(strain, stem_weight, norm_gain, qkv_weight, out_weight, cotangent):
    blocks, features, inverse_rms, normed = embed_strain(strain, stem_weight, norm_gain)
    projected_rows = jnp.dot(normed, qkv_weight, preferred_element_type=jnp.float32).astype(jnp.bfloat16)
    attention_span = QUERY_HEAD_COUNT * HEAD_SIZE
    key_value_width = KEY_VALUE_HEADS * HEAD_SIZE
    shared_portion = QUERY_HEAD_COUNT // KEY_VALUE_HEADS
    query_matrix = projected_rows[:, :attention_span].reshape(N_TM, TOKENS_PER_SHARD, KEY_VALUE_HEADS, shared_portion, HEAD_SIZE)
    local_keys = projected_rows[:, attention_span:attention_span + key_value_width].reshape(N_TM, TOKENS_PER_SHARD, KEY_VALUE_HEADS, HEAD_SIZE)
    local_values = projected_rows[:, attention_span + key_value_width:].reshape(N_TM, TOKENS_PER_SHARD, KEY_VALUE_HEADS, HEAD_SIZE)
    key_rows = jnp.concatenate([jnp.roll(local_keys, 1, axis=0), local_keys], axis=1)
    value_rows = jnp.concatenate([jnp.roll(local_values, 1, axis=0), local_values], axis=1)
    attention_gradient = jnp.dot(cotangent, out_weight, preferred_element_type=jnp.float32).astype(jnp.bfloat16)
    block_gradients = attention_gradient.reshape(N_TM, TOKENS_PER_SHARD, KEY_VALUE_HEADS, shared_portion, HEAD_SIZE)
    mixed, grad_query, key_prev, key_mine, value_prev, value_mine = lax.map(attend_block, (query_matrix, key_rows, value_rows, block_gradients))
    own_grads = jnp.concatenate([grad_query, key_mine, value_mine], axis=-1).reshape(TOKENS, QKV)
    returned = jnp.roll(jnp.concatenate([key_prev, value_prev], axis=-1), -1, axis=0).reshape(TOKENS, 2 * key_value_width)
    mixed_flat = mixed.reshape(TOKENS, attention_span)
    grad_qkv = jnp.dot(normed.T, own_grads, preferred_element_type=jnp.float32)
    grad_qkv = grad_qkv.at[:, attention_span:].add(jnp.dot(normed.T, returned, preferred_element_type=jnp.float32))
    grad_out = jnp.dot(cotangent.T, mixed_flat, preferred_element_type=jnp.float32)
    grad_normed = jnp.dot(own_grads, qkv_weight.T, preferred_element_type=jnp.float32)
    grad_normed = grad_normed + jnp.dot(returned, qkv_weight[:, attention_span:].T, preferred_element_type=jnp.float32)
    scaled = grad_normed * norm_gain
    inner = lax.optimization_barrier(jnp.mean(scaled * features, axis=-1))
    grad_features = inverse_rms[:, None] * scaled - features * (inverse_rms ** 3 * inner)[:, None]
    grad_stem = jnp.einsum('td,cts->dcs', grad_features, blocks, precision=lax.Precision.HIGHEST).reshape(D, PATCH)
    grad_gain = lax.optimization_barrier(jnp.sum(grad_normed * features * inverse_rms[:, None], axis=0))
    return (grad_qkv, grad_out, grad_stem, grad_gain)
```

```python
import jax
import jax.numpy as jnp
from jax import lax
from jax.sharding import PartitionSpec as P

HEAD_SIZE = 64
STRIDE = 16


EPSILON = 1e-05


def passed_along(shard, axis, by):
    devices = lax.axis_size(axis)
    return lax.ppermute(shard, axis, [(i, (i + by) % devices) for i in range(devices)])


def embed_strain(samples, stem_weight, norm_gain):
    channels = samples.shape[0]
    blocks = samples.reshape(channels, -1, STRIDE)
    kernel = stem_weight.reshape(stem_weight.shape[0], channels, STRIDE)
    features = jnp.einsum("cts,dcs->td", blocks, kernel, preferred_element_type=jnp.float32)
    inverse_rms = lax.rsqrt(jnp.mean(features * features, axis=-1) + EPSILON)
    normed = (features * inverse_rms[:, None] * norm_gain).astype(jnp.bfloat16)
    return (features, inverse_rms, normed)


def norm_back(grad_normed, features, inverse_rms, norm_gain, samples):
    scaled = grad_normed * norm_gain
    inner = jnp.mean(scaled * features, axis=-1)
    grad_features = inverse_rms[:, None] * scaled - features * (inverse_rms**3 * inner)[:, None]
    channels = samples.shape[0]
    blocks = samples.astype(jnp.float32).reshape(channels, -1, STRIDE)
    stem_term = jnp.einsum("td,cts->dcs", grad_features, blocks, precision=lax.Precision.HIGHEST)
    stem_term = stem_term.reshape(grad_features.shape[1], -1)
    gain_term = jnp.sum(grad_normed * features * inverse_rms[:, None], axis=0)
    return (stem_term, gain_term)


def attend(query_matrix, key_rows, value_rows, attention_gradient):
    row_count = query_matrix.shape[0]
    group_count = key_rows.shape[1] // HEAD_SIZE
    shared_portion = query_matrix.shape[1] // HEAD_SIZE // group_count
    outputs = [[], [], [], [], [], []]
    for query_group in range(group_count):
        query_cols = slice(
            query_group * shared_portion * HEAD_SIZE, (query_group + 1) * shared_portion * HEAD_SIZE
        )
        head_cols = slice(query_group * HEAD_SIZE, (query_group + 1) * HEAD_SIZE)
        query_heads = query_matrix[:, query_cols].reshape(row_count, shared_portion, HEAD_SIZE)
        key_head = key_rows[:, head_cols]
        value_head = value_rows[:, head_cols]
        grad_heads = attention_gradient[:, query_cols].reshape(row_count, shared_portion, HEAD_SIZE)
        scores = jnp.einsum(
            "tjd,sd->jts", query_heads, key_head, preferred_element_type=jnp.float32
        ) * HEAD_SIZE ** (-0.5)
        row_max = jnp.max(scores, axis=-1, keepdims=True)
        weights = jnp.exp(scores - row_max)
        probs = weights / jnp.sum(weights, axis=-1, keepdims=True)
        probs_low = probs.astype(jnp.bfloat16)
        mixed = jnp.einsum("jts,sd->tjd", probs_low, value_head, preferred_element_type=jnp.float32)
        grad_probs = jnp.einsum(
            "tjd,sd->jts", grad_heads, value_head, preferred_element_type=jnp.float32
        )
        delta = jnp.sum(probs * grad_probs, axis=-1, keepdims=True)
        grad_scores = (probs * (grad_probs - delta)).astype(jnp.bfloat16)
        grad_query = jnp.einsum(
            "jts,sd->tjd", grad_scores, key_head, preferred_element_type=jnp.float32
        ) * HEAD_SIZE ** (-0.5)
        grad_keys = jnp.einsum(
            "jts,tjd->sd", grad_scores, query_heads, preferred_element_type=jnp.float32
        ) * HEAD_SIZE ** (-0.5)
        grad_values = jnp.einsum(
            "jts,tjd->sd", probs_low, grad_heads, preferred_element_type=jnp.float32
        )
        outputs[0].append(mixed.astype(jnp.bfloat16).reshape(row_count, -1))
        outputs[1].append(grad_query.astype(jnp.bfloat16).reshape(row_count, -1))
        outputs[2].append(grad_keys[:row_count].astype(jnp.bfloat16))
        outputs[3].append(grad_keys[row_count:].astype(jnp.bfloat16))
        outputs[4].append(grad_values[:row_count].astype(jnp.bfloat16))
        outputs[5].append(grad_values[row_count:].astype(jnp.bfloat16))
    return tuple((jnp.concatenate(pieces, axis=1) for pieces in outputs))


def contract_rows(left, right):
    return lax.dot_general(
        left, right, (((0,), (0,)), ((), ())), preferred_element_type=jnp.float32
    )


def contract_cols(left, right):
    return lax.dot_general(
        left, right, (((1,), (1,)), ((), ())), preferred_element_type=jnp.float32
    )


def sum_shares(share):
    devices = lax.axis_size("tm")
    pieces = share.astype(jnp.bfloat16).reshape(devices, share.shape[0] // devices, share.shape[1])
    pieces = lax.all_to_all(pieces, "tm", split_axis=0, concat_axis=0, tiled=True)
    return jnp.sum(pieces.astype(jnp.float32), axis=0)


def local(strain, stem_weight, norm_gain, qkv_weight, out_weight, cotangent):
    features, inverse_rms, normed = embed_strain(strain, stem_weight, norm_gain)
    projected_rows = jnp.dot(normed, qkv_weight, preferred_element_type=jnp.float32).astype(
        jnp.bfloat16
    )
    attention_span = out_weight.shape[1]
    own_pairs = projected_rows[:, attention_span:]
    kv_weight = qkv_weight[:, attention_span:]
    prev_pairs = passed_along(own_pairs, "tm", 1)
    key_width = own_pairs.shape[1] // 2
    key_rows = jnp.concatenate([prev_pairs[:, :key_width], own_pairs[:, :key_width]], axis=0)
    value_rows = jnp.concatenate([prev_pairs[:, key_width:], own_pairs[:, key_width:]], axis=0)
    attention_gradient = jnp.dot(cotangent, out_weight, preferred_element_type=jnp.float32).astype(
        jnp.bfloat16
    )
    mixed, grad_query, key_prev, key_mine, value_prev, value_mine = attend(
        projected_rows[:, :attention_span], key_rows, value_rows, attention_gradient
    )
    own_grads = jnp.concatenate([grad_query, key_mine, value_mine], axis=1)
    sent_grads = jnp.concatenate([key_prev, value_prev], axis=1)
    grad_normed = contract_cols(own_grads, qkv_weight)
    returned = passed_along(sent_grads, "tm", -1)
    grad_normed = grad_normed + contract_cols(returned, kv_weight)
    stem_term, gain_term = norm_back(grad_normed, features, inverse_rms, norm_gain, strain)
    result = contract_rows(normed, own_grads)
    result = result.at[:, attention_span:].add(contract_rows(normed, returned))
    grad_out = sum_shares(contract_rows(cotangent, mixed))
    packed = sum_shares(jnp.concatenate([result, stem_term, gain_term[:, None]], axis=1))
    qkv_width = qkv_weight.shape[1]
    return (packed[:, :qkv_width], grad_out, packed[:, qkv_width:-1], packed[:, -1])


def solution(mesh):
    in_specs = (P(None, ("sim", "tm")), P(), P(), P(), P(), P(("sim", "tm"), None))
    out_specs = (
        P(("sim", "tm"), None),
        P(("sim", "tm"), None),
        P(("sim", "tm"), None),
        P(("sim", "tm")),
    )
    return jax.shard_map(local, mesh=mesh, in_specs=in_specs, out_specs=out_specs, check_vma=False)
```

```python
import functools
import math

import jax
import jax.numpy as jnp
from jax import lax
from jax.experimental import pallas as pl
from jax.experimental.pallas import tpu as pltpu
from jax.sharding import PartitionSpec as P

HEAD_SIZE = 64
STRIDE = 16
GROUP_HEADS = 4
GROUPS = 3

EPSILON = 1e-05
BF16 = jnp.bfloat16
F32 = jnp.float32
HEAD_SCALE = HEAD_SIZE ** (-0.5)
EXP_SCALE = HEAD_SCALE * math.log2(math.e)
VMEM_LIMIT = 32 * 2**20


def passed_along(shard, axis, by):
    devices = lax.axis_size(axis)
    return lax.ppermute(shard, axis, [(i, (i + by) % devices) for i in range(devices)])


def nn(left, right):
    return lax.dot_general(left, right, (((1,), (0,)), ((), ())), preferred_element_type=F32)


def nt(left, right):
    return lax.dot_general(left, right, (((1,), (1,)), ((), ())), preferred_element_type=F32)


def attend_kernel(
    group, q_ref, g_ref, prev_ref, own_ref, cot_ref, normed_ref,
    share_ref, dq_ref, prev_grad_ref, own_grad_ref, mixed_ref,
):
    half = own_ref.shape[1] // 2
    rows = own_ref.shape[0]
    key_cols = slice(group * HEAD_SIZE, (group + 1) * HEAD_SIZE)
    value_cols = slice(half + group * HEAD_SIZE, half + (group + 1) * HEAD_SIZE)
    keys = jnp.concatenate([prev_ref[:, key_cols], own_ref[:, key_cols]], axis=0)
    values = jnp.concatenate([prev_ref[:, value_cols], own_ref[:, value_cols]], axis=0)
    keys_t = keys.T
    values_t = jnp.concatenate([values.T, jnp.ones((16, values.shape[0]), BF16)], axis=0)
    grad_keys = None
    grad_values = None
    for head in range(GROUP_HEADS):
        head_rows = slice(head * HEAD_SIZE, (head + 1) * HEAD_SIZE)
        query = q_ref[head_rows, :]
        grad = g_ref[head_rows, :]
        scores = nn(keys, query)
        top = jnp.max(scores, axis=0, keepdims=True)
        weights = jnp.exp2(scores * EXP_SCALE - top * EXP_SCALE)
        weights_low = weights.astype(BF16)
        mixed = nn(values_t, weights_low)
        inverse = 1.0 / mixed[HEAD_SIZE : HEAD_SIZE + 1]
        mixed = mixed[:HEAD_SIZE] * inverse
        mixed_ref[head_rows, :] = mixed.astype(BF16)
        grad_wide = grad.astype(F32)
        delta = jnp.sum(mixed * grad_wide, axis=0, keepdims=True)
        grad_scores = (weights * (nn(values, grad) - delta)).astype(BF16)
        scaled = inverse * HEAD_SCALE
        dq_ref[head_rows, :] = (nn(keys_t, grad_scores) * scaled).astype(BF16)
        key_part = nt(grad_scores, (query.astype(F32) * scaled).astype(BF16))
        value_part = nt(weights_low, (grad_wide * inverse).astype(BF16))
        grad_keys = key_part if grad_keys is None else grad_keys + key_part
        grad_values = value_part if grad_values is None else grad_values + value_part
    both = jnp.concatenate([grad_keys, grad_values], axis=1).astype(BF16)
    prev_grad_ref[...] = both[:rows]
    own_grad_ref[...] = both[rows:]
    width = mixed_ref.shape[0]
    share_ref[:, :width] = nt(cot_ref[...], mixed_ref[...]).astype(BF16)
    share_ref[:, width:] = nt(normed_ref[...], dq_ref[...]).astype(BF16)


def whole(array):
    return pl.BlockSpec(array.shape, lambda step: (0,) * array.ndim)


def attend_group(group, q_t, g_t, prev_pairs, own_pairs, cot_t, normed_t):
    tokens = own_pairs.shape[0]
    width = GROUP_HEADS * HEAD_SIZE
    outs = [
        jax.ShapeDtypeStruct((cot_t.shape[0], 2 * width), BF16),
        jax.ShapeDtypeStruct((width, tokens), BF16),
        jax.ShapeDtypeStruct((tokens, 2 * HEAD_SIZE), BF16),
        jax.ShapeDtypeStruct((tokens, 2 * HEAD_SIZE), BF16),
    ]
    block = pl.BlockSpec((width, tokens), lambda step: (group, 0))
    return pl.pallas_call(
        functools.partial(attend_kernel, group),
        grid=(1,),
        in_specs=[block, block] + [whole(a) for a in (prev_pairs, own_pairs, cot_t, normed_t)],
        out_specs=[whole(a) for a in outs],
        out_shape=outs,
        scratch_shapes=[pltpu.VMEM((width, tokens), BF16)],
        compiler_params=pltpu.CompilerParams(vmem_limit_bytes=VMEM_LIMIT),
        cost_estimate=pl.CostEstimate(
            flops=2 * 7 * 4 * 512 * 1024 * 64, bytes_accessed=5 * 2**20, transcendentals=2**21
        ),
        name=f"attend_{group}",
    )(q_t, g_t, prev_pairs, own_pairs, cot_t, normed_t)


def tail_kernel(
    dq0, dq1, dq2, own0, own1, own2, back0, back1, back2,
    weight_ref, patches_ref, stem_ref, gain_ref, normed_ref, out_ref,
):
    def joined(parts):
        parts = [part[...] for part in parts]
        return jnp.concatenate(
            [part[:, :HEAD_SIZE] for part in parts] + [part[:, HEAD_SIZE:] for part in parts], axis=1
        )

    own = joined((own0, own1, own2))
    back = joined((back0, back1, back2))
    dq = jnp.concatenate([dq0[...], dq1[...], dq2[...]], axis=0)
    span = dq.shape[0]
    patches = patches_ref[...]
    features = nt(stem_ref[...], patches)
    inverse_rms = lax.rsqrt(jnp.mean(features * features, axis=0, keepdims=True) + EPSILON)
    kv_weight = weight_ref[:, span:]
    grad_normed = nn(weight_ref[:, :span], dq) + nt(kv_weight, own) + nt(kv_weight, back)
    scaled = grad_normed * gain_ref[...]
    inner = jnp.mean(scaled * features, axis=0, keepdims=True)
    gain_term = jnp.sum(grad_normed * features * inverse_rms, axis=1, keepdims=True)
    grad_features = inverse_rms * scaled - features * (inverse_rms**3 * inner)
    high = grad_features.astype(BF16)
    low = (grad_features - high.astype(F32)).astype(BF16)
    stem_term = nn(high, patches) + nn(low, patches)
    normed = normed_ref[...]
    kv_term = nn(normed, own) + nn(normed, back)
    kv_width = kv_term.shape[1]
    out_ref[:, :kv_width] = kv_term.astype(BF16)
    spare = jnp.zeros((span, out_ref.shape[1] - kv_width - stem_term.shape[1] - 1), F32)
    out_ref[:, kv_width:] = jnp.concatenate([stem_term, gain_term, spare], axis=1).astype(BF16)


def tail(dqs, owns, backs, weight, patches, stem, gain, normed_t):
    out = jax.ShapeDtypeStruct((normed_t.shape[0], 512), BF16)
    args = (*dqs, *owns, *backs, weight, patches, stem, gain, normed_t)
    return pl.pallas_call(
        tail_kernel,
        grid=(1,),
        in_specs=[whole(a) for a in args],
        out_specs=whole(out),
        out_shape=out,
        compiler_params=pltpu.CompilerParams(vmem_limit_bytes=VMEM_LIMIT),
        name="tail",
    )(*args)


def spread_shares(share):
    devices = lax.axis_size("tm")
    pieces = share.reshape(devices, share.shape[0] // devices, share.shape[1])
    return lax.all_to_all(pieces, "tm", split_axis=0, concat_axis=0, tiled=True)


def summed(pieces):
    return jnp.sum(pieces.astype(F32), axis=0)


def local(strain, stem_weight, norm_gain, qkv_weight, out_weight, cotangent):
    channels = strain.shape[0]
    span = out_weight.shape[1]
    patches = strain.reshape(channels, -1, STRIDE).transpose(1, 0, 2).reshape(-1, channels * STRIDE)
    features = nt(patches, stem_weight)
    inverse_rms = lax.rsqrt(jnp.mean(features * features, axis=-1, keepdims=True) + EPSILON)
    normed = (features * inverse_rms * norm_gain).astype(BF16)
    own_pairs = nn(normed, qkv_weight[:, span:]).astype(BF16)
    prev_pairs = passed_along(own_pairs, "tm", 1)
    q_t = lax.dot_general(
        qkv_weight[:, :span], normed, (((0,), (1,)), ((), ())), preferred_element_type=F32
    ).astype(BF16)
    g_t = lax.dot_general(
        out_weight, cotangent, (((0,), (1,)), ((), ())), preferred_element_type=F32
    ).astype(BF16)
    cot_t = cotangent.T
    normed_t = normed.T
    dqs, owns, backs, sums = [], [], [], []
    for group in range(GROUPS):
        share, dq, prev_grad, own_grad = attend_group(
            group, q_t, g_t, prev_pairs, own_pairs, cot_t, normed_t
        )
        sums.append(spread_shares(share))
        dqs.append(dq)
        owns.append(own_grad)
        backs.append(passed_along(prev_grad, "tm", -1))
    packed = tail(
        dqs, owns, backs, qkv_weight, patches, stem_weight, norm_gain[:, None], normed_t
    )
    sums = [summed(s) for s in sums]
    last = summed(spread_shares(packed))
    width = GROUP_HEADS * HEAD_SIZE
    kv_width = qkv_weight.shape[1] - span
    patch = stem_weight.shape[1]
    grad_qkv = jnp.concatenate([s[:, width:] for s in sums] + [last[:, :kv_width]], axis=1)
    grad_out = jnp.concatenate([s[:, :width] for s in sums], axis=1)
    return (
        grad_qkv,
        grad_out,
        last[:, kv_width : kv_width + patch],
        last[:, kv_width + patch],
    )


def solution(mesh):
    in_specs = (P(None, ("sim", "tm")), P(), P(), P(), P(), P(("sim", "tm"), None))
    out_specs = (
        P(("sim", "tm"), None),
        P(("sim", "tm"), None),
        P(("sim", "tm"), None),
        P(("sim", "tm")),
    )
    return jax.shard_map(local, mesh=mesh, in_specs=in_specs, out_specs=out_specs, check_vma=False)
```
